32 devices in a mesh: dp: 4 (over y, x), expert: 4 (over z), tensor: 2 (over core).
Axes of the slice: x: 2, y: 2, z: 4, core: 2. Of those that a mesh axis runs over, the one named last changes fastest.
Arguments:
- activations: bfloat16 [2048, 2880], P(('dp', 'expert'), 'tensor'), may hold values from -6 to 6
- output_gradient: bfloat16 [2048, 2880], P(('dp', 'expert'), 'tensor'), may hold values from -6 to 6
- combine_weight: float32 [2048, 4], P(('dp', 'expert')), may hold values from 0.05 to 0.6
- token_experts: int32 [2048, 4], P(('dp', 'expert')), may hold values from 0 to 3, as said below
- gate_up_weight: bfloat16 [4, 2, 1440, 2880], P('expert', None, 'tensor'), may hold values from -0.109375 to 0.109375
- gate_up_channel_scale: float32 [4, 2, 1440], P('expert', None, 'tensor'), may hold values from 0.5 to 2
- down_weight: bfloat16 [4, 1440, 2880], P('expert', 'tensor'), may hold values from -0.15625 to 0.15625
- down_channel_scale: float32 [4, 2880], P('expert'), may hold values from 0.5 to 2
- adapter_input_first: bfloat16 [4, 2880, 32], P('expert'), may hold values from -0.109375 to 0.109375
- adapter_input_second: bfloat16 [4, 32, 2, 1440], P('expert', None, None, 'tensor'), may hold values from -0.5 to 0.5
- adapter_down_first: bfloat16 [4, 1440, 32], P('expert', 'tensor'), may hold values from -0.15625 to 0.15625
- adapter_down_second: bfloat16 [4, 32, 2880], P('expert'), may hold values from -0.5 to 0.5
Outputs:
- input_grad: bfloat16 [2048, 2880], P(('dp', 'expert'), 'tensor')
- grad_a_in: float32 [4, 2880, 32], P('expert', 'tensor')
- grad_b_in: float32 [4, 32, 2, 1440], P('expert', None, None, 'tensor')
- grad_a_down: float32 [4, 1440, 32], P('expert', 'tensor')
- grad_b_down: float32 [4, 32, 2880], P('expert', None, 'tensor')
The draws below stay inside these ranges and needn't reach their ends.
Inputs may be any that keep to these rules, and one draw needn't show every extreme that they name: `token_experts`: each row names 4 different experts.
All inputs are finite; a program needn't handle non-finite values.
Results may differ from the reference program's by a relative error of at most 0.02.
Values may be sent and summed in bfloat16 or wider, within the bound.
A program may use at most 128 MiB of HBM per device.

```python
import math
import jax
import jax.numpy as jnp
from jax import lax

MODEL_WIDTH = 2880
HIDDEN_HALF = 1440
ADAPTER_RANK = 32
TOP = 4
EXP_DEV = 1
TOK_DEV = 128
EXPERT_TOTAL = 4
TOKEN_TOTAL = 2048
CAP = 128
N_TENSOR = 2


def draw_token_experts(key, part):
    key = jax.random.fold_in(key, 5)
    keys = jax.random.split(key, 4)
    blocks = TOKEN_TOTAL // TOK_DEV
    per_group = EXPERT_TOTAL // EXP_DEV
    groups = blocks // per_group
    random_jitter = jax.random.randint(keys[0], (TOKEN_TOTAL, EXPERT_TOTAL), 0, 65536, dtype=jnp.int32)
    preference = jax.random.randint(keys[1], (EXPERT_TOTAL,), 0, 32768, dtype=jnp.int32)
    hot_group = jax.random.randint(keys[2], (groups,), 0, EXPERT_TOTAL, dtype=jnp.int32)
    hot_expert = jnp.repeat(hot_group, per_group * TOK_DEV)
    order = jax.random.randint(keys[3], (blocks, TOK_DEV), 0, 1 << 20, dtype=jnp.int32) * TOK_DEV + jnp.arange(TOK_DEV, dtype=jnp.int32)[None, :]
    ranking = jnp.argsort(jnp.argsort(order, axis=1), axis=1).reshape(TOKEN_TOTAL)
    selected_experts = ranking < min(CAP + 8, TOK_DEV)
    column_position = jnp.arange(EXPERT_TOTAL, dtype=jnp.int32)[None, :]
    extra_amount = jnp.where(selected_experts[:, None] & (column_position == hot_expert[:, None]), 1 << 18, 0)
    expert_score = (random_jitter + preference[None, :] + extra_amount) * EXPERT_TOTAL + column_position
    return lax.top_k(expert_score, TOP)[1].astype(jnp.int32)


def block_levels(stream_key, shape, cuts, least, top_value):
    level = 1.0
    for dim, blocks in cuts:
        heights = jax.random.uniform(jax.random.fold_in(jax.random.fold_in(stream_key, 6), dim), (blocks,), jnp.float32, least / len(cuts), top_value / len(cuts))
        level = level * jnp.repeat(jnp.exp(heights), shape[dim] // blocks).reshape((-1,) + (1,) * (len(shape) - 1 - dim))
    return level


def normal_values(key, dims, deviation, limit, shards=(), held_as=jnp.bfloat16):
    loudness = block_levels(key, dims, shards, -0.22, 0.18) if shards else 1.0
    array = jax.random.normal(key, dims, jnp.float32) * deviation * loudness
    return jnp.minimum(jnp.maximum(array, -limit), limit).astype(held_as)


def setup_inputs(seed: int = 0) -> dict:
    splits = jax.random.split(jax.random.key(seed), 13)
    activations = normal_values(splits[0], (TOKEN_TOTAL, MODEL_WIDTH), 1.0, 6.0, ((0, 16), (1, 2)))
    output_gradient = normal_values(splits[1], (TOKEN_TOTAL, MODEL_WIDTH), 1.0, 6.0, ((0, 16), (1, 2)))
    combine_weight = jnp.clip(0.05 + 0.55 * jax.random.uniform(splits[2], (TOKEN_TOTAL, TOP), jnp.float32) ** block_levels(splits[2], (TOKEN_TOTAL, TOP), ((0, 16),), -0.2, 0.2), 0.05, 0.6)
    token_experts = draw_token_experts(jax.random.fold_in(splits[12], 71), 0)
    gate_up_weight = normal_values(splits[4], (EXPERT_TOTAL, 2, HIDDEN_HALF, MODEL_WIDTH), MODEL_WIDTH ** -0.5, 0.109375, ((0, 4), (2, 2)))
    gate_up_channel_scale = jnp.clip(jnp.exp(math.log(2.0) - 1.3862944 * jax.random.uniform(splits[5], (EXPERT_TOTAL, 2, HIDDEN_HALF), jnp.float32) ** block_levels(splits[5], (EXPERT_TOTAL, 2, HIDDEN_HALF), ((0, 4), (2, 2)), -0.2, 0.2)), 0.5, 2.0)
    down_weight = normal_values(splits[6], (EXPERT_TOTAL, HIDDEN_HALF, MODEL_WIDTH), HIDDEN_HALF ** -0.5, 0.15625, ((0, 4), (1, 2)))
    down_channel_scale = jnp.clip(jnp.exp(math.log(2.0) - 1.3862944 * jax.random.uniform(splits[7], (EXPERT_TOTAL, MODEL_WIDTH), jnp.float32) ** block_levels(splits[7], (EXPERT_TOTAL, MODEL_WIDTH), ((0, 4),), -0.2, 0.2)), 0.5, 2.0)
    adapter_input_first = normal_values(splits[8], (EXPERT_TOTAL, MODEL_WIDTH, ADAPTER_RANK), MODEL_WIDTH ** -0.5, 0.109375, ((0, 4),))
    adapter_input_second = normal_values(splits[9], (EXPERT_TOTAL, ADAPTER_RANK, 2, HIDDEN_HALF), (4 * ADAPTER_RANK) ** -0.5, 0.5, ((0, 4), (3, 2)))
    adapter_down_first = normal_values(splits[10], (EXPERT_TOTAL, HIDDEN_HALF, ADAPTER_RANK), HIDDEN_HALF ** -0.5, 0.15625, ((0, 4), (1, 2)))
    adapter_down_second = normal_values(splits[11], (EXPERT_TOTAL, ADAPTER_RANK, MODEL_WIDTH), (4 * ADAPTER_RANK) ** -0.5, 0.5, ((0, 4),))
    return dict(activations=activations, output_gradient=output_gradient, combine_weight=combine_weight, token_experts=token_experts, gate_up_weight=gate_up_weight, gate_up_channel_scale=gate_up_channel_scale, down_weight=down_weight, down_channel_scale=down_channel_scale, adapter_input_first=adapter_input_first, adapter_input_second=adapter_input_second, adapter_down_first=adapter_down_first, adapter_down_second=adapter_down_second)


ALPHA = 1.702
ADAPTER_SCALE = 2.0


def reference(activations, output_gradient, combine_weight, token_experts, gate_up_weight, gate_up_channel_scale, down_weight, down_channel_scale, adapter_input_first, adapter_input_second, adapter_down_first, adapter_down_second):
    single_float = jnp.float32
    brain_float_half = jnp.bfloat16
    blocks = TOKEN_TOTAL // TOK_DEV
    width = blocks * CAP
    flat_experts = token_experts.reshape(blocks, TOK_DEV * TOP)
    onehot = (flat_experts[:, :, None] == jnp.arange(EXPERT_TOTAL, dtype=jnp.int32)[None, None, :]).astype(jnp.int32)
    before = (jnp.cumsum(onehot, axis=1, dtype=jnp.int32) - onehot).astype(jnp.int32)
    counted = jnp.sum(before * onehot, axis=2, dtype=jnp.int32).astype(jnp.int32)
    slot_positions = jnp.where(counted < CAP, counted, -1).reshape(TOKEN_TOTAL, TOP).astype(jnp.int32)
    token = jnp.arange(TOKEN_TOTAL, dtype=jnp.int32)[:, None]
    live = slot_positions >= 0
    where_to = jnp.where(live, (token // TOK_DEV) * CAP + slot_positions, width).astype(jnp.int32)
    assign = (token * TOP + jnp.arange(TOP, dtype=jnp.int32)[None, :]).astype(jnp.int32)
    lookup_table = jnp.full((EXPERT_TOTAL, width), -1, jnp.int32).at[token_experts, where_to].set(assign, mode="drop")
    flat_weight = combine_weight.reshape(-1)
    group = HIDDEN_HALF // N_TENSOR

    def single_expert(total_amount, inputs):
        row_ids, gate_up_w, gate_up_s, down_matrix, down_s, input_first_factor, input_second_factor, down_first_factor, b_down = inputs
        valid = row_ids >= 0
        source = jnp.where(valid, row_ids, 0)
        tok = source // TOP
        input_rows = jnp.where(valid[:, None], activations[tok], jnp.zeros((), brain_float_half))
        dy_rows = jnp.where(valid[:, None], output_gradient[tok], jnp.zeros((), brain_float_half))
        weight = jnp.where(valid, flat_weight[source], jnp.zeros((), single_float))
        output_gradient_value = (weight[:, None] * dy_rows.astype(single_float)).astype(brain_float_half)
        gate_scores = (output_gradient_value.astype(single_float) * down_s[None, :]).astype(brain_float_half)
        adapter_input_rows = jnp.dot(input_rows, input_first_factor, preferred_element_type=single_float).astype(brain_float_half)
        gate_values = jnp.dot(input_rows, gate_up_w[0].T, preferred_element_type=single_float) * gate_up_s[0][None, :]
        gate_values = gate_values + ADAPTER_SCALE * jnp.dot(adapter_input_rows, input_second_factor[:, 0, :], preferred_element_type=single_float)
        up_values = jnp.dot(input_rows, gate_up_w[1].T, preferred_element_type=single_float) * gate_up_s[1][None, :]
        up_values = up_values + ADAPTER_SCALE * jnp.dot(adapter_input_rows, input_second_factor[:, 1, :], preferred_element_type=single_float)
        sig = jax.nn.sigmoid(ALPHA * gate_values)
        glu = gate_values * sig
        hidden_units = ((up_values + 1.0) * glu).astype(brain_float_half)
        down_adapter = jnp.dot(hidden_units, down_first_factor, preferred_element_type=single_float).astype(brain_float_half)
        backward_adapter = jnp.dot(output_gradient_value, b_down.T, preferred_element_type=single_float).astype(brain_float_half)
        hidden_delta = jnp.dot(gate_scores, down_matrix.T, preferred_element_type=single_float) + ADAPTER_SCALE * jnp.dot(backward_adapter, down_first_factor.T, preferred_element_type=single_float)
        d_up = hidden_delta * glu
        d_gate = hidden_delta * (up_values + 1.0) * sig * (1.0 + ALPHA * gate_values * (1.0 - sig))
        dz = jnp.stack([d_gate, d_up], axis=1)
        adapter_mid_gradient = dz.astype(brain_float_half)
        dzs = (dz * gate_up_s[None, :, :]).astype(brain_float_half)
        input_adapter = jnp.einsum("ndy,tdy->nt", adapter_mid_gradient.astype(single_float), input_second_factor.astype(single_float)).astype(brain_float_half)
        summed_values = jnp.zeros((input_rows.shape[0], MODEL_WIDTH), single_float)
        for part in range(N_TENSOR):
            piece = jnp.einsum("rjf,jfd->rd", dzs[:, :, part * group:(part + 1) * group].astype(single_float), gate_up_w[:, part * group:(part + 1) * group, :].astype(single_float))
            rounded = lax.optimization_barrier(piece.astype(brain_float_half))
            summed_values = summed_values + rounded.astype(single_float)
        input_gradient_rows = (summed_values + ADAPTER_SCALE * jnp.dot(input_adapter, input_first_factor.T, preferred_element_type=single_float)).astype(brain_float_half)
        total_amount = total_amount.at[tok].add(jnp.where(valid[:, None], input_gradient_rows.astype(single_float), jnp.zeros((), single_float)))
        input_first_gradient = ADAPTER_SCALE * jnp.dot(input_rows.T, input_adapter, preferred_element_type=single_float)
        input_second_gradient = ADAPTER_SCALE * jnp.einsum("hp,hwl->pwl", adapter_input_rows.astype(single_float), adapter_mid_gradient.astype(single_float))
        down_first_gradient = ADAPTER_SCALE * jnp.dot(hidden_units.T, backward_adapter, preferred_element_type=single_float)
        down_second_gradient = ADAPTER_SCALE * jnp.dot(down_adapter.T, output_gradient_value, preferred_element_type=single_float)
        return total_amount, (input_first_gradient, input_second_gradient, down_first_gradient, down_second_gradient)

    total_amount, gradient_results = lax.scan(single_expert, jnp.zeros((TOKEN_TOTAL, MODEL_WIDTH), single_float), (lookup_table, gate_up_weight, gate_up_channel_scale, down_weight, down_channel_scale, adapter_input_first, adapter_input_second, adapter_down_first, adapter_down_second))
    return (total_amount.astype(brain_float_half), gradient_results[0], gradient_results[1], gradient_results[2], gradient_results[3])
```

```python
import jax
import jax.numpy as jnp
from jax import lax
from jax.sharding import PartitionSpec as P

ALPHA = 1.702
ADAPTER_SCALE = 2.0


def contract_product(left, right, left_dim, right_dim):
    return lax.dot_general(
        left, right, (((left_dim,), (right_dim,)), ((), ())), preferred_element_type=jnp.float32
    )


def shards(
    activations,
    output_gradient,
    combine_weight,
    token_experts,
    gate_up_weight,
    gate_up_channel_scale,
    down_weight,
    down_channel_scale,
    adapter_input_first,
    adapter_input_second,
    adapter_down_first,
    adapter_down_second,
):
    single_float = jnp.float32
    brain_float_half = jnp.bfloat16
    n_expert = lax.axis_size("expert")
    local_count = gate_up_weight.shape[0]
    experts_all = local_count * n_expert
    tok_rows = activations.shape[0]
    top_count = token_experts.shape[1]
    capacity = min(tok_rows * top_count * 11 // (8 * experts_all), tok_rows)
    gradient_slice = activations.shape[1]
    slots_all = experts_all * capacity
    dense = experts_all == top_count and capacity == tok_rows
    if dense:
        expert_ids = jnp.arange(experts_all, dtype=jnp.int32)
        token_weight = jnp.sum(
            jnp.where(
                token_experts[:, :, None] == expert_ids[None, None, :],
                combine_weight[:, :, None],
                0.0,
            ),
            axis=1,
        )
        half_x = lax.all_gather(activations, "expert", axis=0, tiled=True)
        half_dy = lax.all_gather(output_gradient, "expert", axis=0, tiled=True)
        weights = lax.all_gather(token_weight, "expert", axis=0, tiled=True)
        mine = lax.axis_index("expert")
        recv_w = lax.dynamic_slice_in_dim(weights, mine, 1, 1).reshape(1, -1)
        recv_x = lax.all_gather(half_x, "tensor", axis=1, tiled=True)[None]
        recv_dy = lax.all_gather(half_dy, "tensor", axis=1, tiled=True)[None]
    else:
        flat_experts = token_experts.reshape(tok_rows * top_count)
        onehot = (flat_experts[:, None] == jnp.arange(experts_all, dtype=jnp.int32)[None, :]).astype(
            jnp.int32
        )
        before = jnp.cumsum(onehot, axis=0, dtype=jnp.int32) - onehot
        counted = jnp.sum(before * onehot, axis=1, dtype=jnp.int32)
        slot_positions = jnp.where(counted < capacity, counted, -1).reshape(tok_rows, top_count)
        target = jnp.where(slot_positions >= 0, token_experts * capacity + slot_positions, -1)
        matched = target[None, :, :] == jnp.arange(slots_all, dtype=jnp.int32)[:, None, None]
        placing = jnp.any(matched, axis=2).astype(brain_float_half)
        slot_weight = jnp.sum(jnp.where(matched, combine_weight[None, :, :], 0.0), axis=(1, 2)).reshape(
            experts_all, capacity
        )
        whole_x, whole_dy = (
            lax.all_gather(activations, "tensor", axis=1, tiled=True),
            lax.all_gather(output_gradient, "tensor", axis=1, tiled=True),
        )
        d_whole = whole_x.shape[1]
        sent_x = (
            jnp.dot(placing, whole_x, preferred_element_type=single_float)
            .astype(brain_float_half)
            .reshape(experts_all, capacity, d_whole)
        )
        sent_dy = (
            jnp.dot(placing, whole_dy, preferred_element_type=single_float)
            .astype(brain_float_half)
            .reshape(experts_all, capacity, d_whole)
        )
        recv_x, recv_dy, recv_w = (
            lax.all_to_all(sent_x, "expert", split_axis=0, concat_axis=1, tiled=True),
            lax.all_to_all(sent_dy, "expert", split_axis=0, concat_axis=1, tiled=True),
            lax.all_to_all(
                slot_weight.astype(jnp.bfloat16), "expert", split_axis=0, concat_axis=1, tiled=True
            ).astype(slot_weight.dtype),
        )
    gradient_start = lax.axis_index("tensor") * gradient_slice
    gradient_listing = ([], [], [], [])
    input_rows = recv_x[0]
    dy_rows = recv_dy[0]
    gradient_rows = (recv_w[0][:, None] * dy_rows.astype(single_float)).astype(brain_float_half)
    scaled_gradient = (gradient_rows.astype(single_float) * down_channel_scale[0][None, :]).astype(
        brain_float_half
    )
    adapter_input_rows = jnp.dot(
        input_rows, adapter_input_first[0], preferred_element_type=single_float
    ).astype(brain_float_half)
    gate_values = (
        contract_product(input_rows, gate_up_weight[0, 0], 1, 1)
        * gate_up_channel_scale[0, 0][None, :]
    )
    gate_values = gate_values + ADAPTER_SCALE * jnp.dot(
        adapter_input_rows, adapter_input_second[0][:, 0, :], preferred_element_type=single_float
    )
    up_activation = (
        contract_product(input_rows, gate_up_weight[0, 1], 1, 1)
        * gate_up_channel_scale[0, 1][None, :]
    )
    up_activation = up_activation + ADAPTER_SCALE * jnp.dot(
        adapter_input_rows, adapter_input_second[0][:, 1, :], preferred_element_type=single_float
    )
    sig = jax.nn.sigmoid(ALPHA * gate_values)
    glu = gate_values * sig
    hidden_units = ((up_activation + 1.0) * glu).astype(brain_float_half)
    down_portion = jnp.dot(hidden_units, adapter_down_first[0], preferred_element_type=single_float)
    down_sum = lax.psum(down_portion.astype(jnp.bfloat16), "tensor").astype(jnp.float32)
    backward_adapter = contract_product(gradient_rows, adapter_down_second[0], 1, 1).astype(
        brain_float_half
    )
    hidden_gradient = contract_product(
        scaled_gradient, down_weight[0], 1, 1
    ) + ADAPTER_SCALE * contract_product(backward_adapter, adapter_down_first[0], 1, 1)
    d_up = hidden_gradient * glu
    d_gate = (
        hidden_gradient * (up_activation + 1.0) * sig * (1.0 + ALPHA * gate_values * (1.0 - sig))
    )
    d_both = jnp.stack([d_gate, d_up], axis=1)
    adapter_mid_gradient = d_both.astype(brain_float_half)
    dz_scaled = (d_both * gate_up_channel_scale[0][None, :, :]).astype(brain_float_half)
    input_portion = jnp.einsum(
        "ndy,tdy->nt",
        adapter_mid_gradient,
        adapter_input_second[0],
        preferred_element_type=single_float,
    )
    in_sum = lax.psum(input_portion.astype(jnp.bfloat16), "tensor").astype(jnp.float32)
    down_adapter = down_sum.astype(brain_float_half)
    input_adapter = in_sum.astype(brain_float_half)
    partial_value = jnp.einsum(
        "rjf,jfd->rd", dz_scaled, gate_up_weight[0], preferred_element_type=single_float
    )
    summed_values = lax.psum_scatter(
        partial_value.astype(jnp.bfloat16), "tensor", scatter_dimension=1, tiled=True
    ).astype(jnp.float32)
    input_first_rows = lax.dynamic_slice_in_dim(
        adapter_input_first[0], gradient_start, gradient_slice, 0
    )
    input_gradient_rows = (
        summed_values + ADAPTER_SCALE * contract_product(input_adapter, input_first_rows, 1, 1)
    ).astype(brain_float_half)
    dx_list = [input_gradient_rows]
    input_columns = lax.dynamic_slice_in_dim(input_rows, gradient_start, gradient_slice, 1)
    gradient_columns = lax.dynamic_slice_in_dim(gradient_rows, gradient_start, gradient_slice, 1)
    gradient_listing[0].append(ADAPTER_SCALE * contract_product(input_columns, input_adapter, 0, 0))
    gradient_listing[1].append(
        ADAPTER_SCALE
        * jnp.einsum(
            "hp,hwl->pwl",
            adapter_input_rows,
            adapter_mid_gradient,
            preferred_element_type=single_float,
        )
    )
    gradient_listing[2].append(
        ADAPTER_SCALE * contract_product(hidden_units, backward_adapter, 0, 0)
    )
    gradient_listing[3].append(
        ADAPTER_SCALE * contract_product(down_adapter, gradient_columns, 0, 0)
    )
    stacked = tuple((jnp.stack(items, axis=0) for items in gradient_listing))
    input_first_gradient, input_second_gradient, down_first_gradient, down_second_gradient = (
        lax.psum(stacked[0].astype(jnp.bfloat16), "dp").astype(jnp.float32),
        lax.psum(stacked[1].astype(jnp.bfloat16), "dp").astype(jnp.float32),
        lax.psum(stacked[2].astype(jnp.bfloat16), "dp").astype(jnp.float32),
        lax.psum(stacked[3].astype(jnp.bfloat16), "dp").astype(jnp.float32),
    )
    if dense:
        input_grad = lax.psum_scatter(
            dx_list[0], "expert", scatter_dimension=0, tiled=True
        )
    else:
        returned = lax.all_to_all(
            jnp.stack(dx_list, axis=0), "expert", split_axis=1, concat_axis=0, tiled=True
        )
        flat_rows = returned.reshape(slots_all, gradient_slice)
        input_grad = contract_product(placing, flat_rows, 0, 0).astype(brain_float_half)
    return (
        input_grad,
        input_first_gradient,
        input_second_gradient,
        down_first_gradient,
        down_second_gradient,
    )


def solution(mesh):
    placed = (
        P(("dp", "expert"), "tensor"),
        P(("dp", "expert"), "tensor"),
        P(("dp", "expert"), None),
        P(("dp", "expert"), None),
        P("expert", None, "tensor", None),
        P("expert", None, "tensor"),
        P("expert", "tensor", None),
        P("expert", None),
        P("expert", None, None),
        P("expert", None, None, "tensor"),
        P("expert", "tensor", None),
        P("expert", None, None),
    )
    return jax.shard_map(
        shards,
        mesh=mesh,
        in_specs=placed,
        out_specs=(
            P(("dp", "expert"), "tensor"),
            P("expert", "tensor", None),
            P("expert", None, None, "tensor"),
            P("expert", "tensor", None),
            P("expert", None, "tensor"),
        ),
        check_vma=False,
    )
```

```python
import functools

import jax
import jax.numpy as jnp
from jax import lax
from jax.experimental import pallas as pl
from jax.experimental.pallas import tpu as pltpu
from jax.sharding import PartitionSpec as P

ALPHA = 1.702
ADAPTER_SCALE = 2.0


def contract_product(left, right, left_dim, right_dim):
    return lax.dot_general(
        left, right, (((left_dim,), (right_dim,)), ((), ())), preferred_element_type=jnp.float32
    )


MESH = pl.DeviceIdType.MESH


def remote(src, dst, send, recv, **where):
    return pltpu.make_async_remote_copy(
        src_ref=src, dst_ref=dst, send_sem=send, recv_sem=recv, device_id=where, device_id_type=MESH
    )


def gather_kernel(
    n, x_ref, dy_ref, w_ref, x_out, dy_out, w_out, held,
    line_send, line_recv, pair_send, pair_recv, w_send, w_recv,
):
    e = lax.axis_index("expert")
    c = lax.axis_index("tensor")
    rows, width = x_ref.shape
    barrier = pltpu.get_barrier_semaphore()
    for j in range(1, n):
        pl.semaphore_signal(
            barrier, inc=1, device_id={"expert": lax.rem(e + j, n)}, device_id_type=MESH
        )
    pl.semaphore_signal(barrier, inc=1, device_id={"tensor": 1 - c}, device_id_type=MESH)
    pl.semaphore_wait(barrier, n)

    def piece(a, s):
        return held.at[a, s, c]

    def block(direction, k):
        return e - k if direction == 0 else e + k

    def arrives(direction, k):
        return e >= k if direction == 0 else e + k <= n - 1

    def goes_on(direction):
        return e < n - 1 if direction == 0 else e > 0

    def line(a, direction, k):
        s = block(direction, k)
        return remote(
            piece(a, s), piece(a, s), line_send.at[a, direction, k], line_recv.at[a, direction, k],
            expert=e + 1 if direction == 0 else e - 1,
        )

    def line_in(a, direction, k):
        s = block(direction, k)
        return remote(
            piece(a, s), piece(a, s),
            line_send.at[a, direction, k - 1], line_recv.at[a, direction, k - 1],
            expert=e - 1 if direction == 0 else e + 1,
        )

    def pair(a, s, slot):
        return remote(
            piece(a, s), piece(a, s), pair_send.at[a, slot], pair_recv.at[a, slot], tensor=1 - c
        )

    def pair_in(a, s, slot):
        other = held.at[a, s, 1 - c]
        return remote(other, other, pair_send.at[a, slot], pair_recv.at[a, slot], tensor=1 - c)

    def own(a):
        for direction in range(2):
            @pl.when(goes_on(direction))
            def _():
                line(a, direction, 0).start()
        pair(a, e, 0).start()

    def hop(a, k):
        for direction in range(2):
            @pl.when(arrives(direction, k))
            def _():
                line_in(a, direction, k).wait_recv()
                if k < n - 1:
                    @pl.when(goes_on(direction))
                    def _():
                        line(a, direction, k).start()
                pair(a, block(direction, k), direction * (n - 1) + k).start()

    def settle(a, out):
        def lay(s):
            where = pl.ds(pl.multiple_of(s * rows, rows), rows)
            out[where, :] = jnp.concatenate([held[a, s, 0], held[a, s, 1]], axis=1)

        pair_in(a, e, 0).wait_recv()
        lay(e)
        for k in range(1, n):
            for direction in range(2):
                @pl.when(arrives(direction, k))
                def _():
                    s = block(direction, k)
                    pair_in(a, s, direction * (n - 1) + k).wait_recv()
                    lay(s)

    held[0, e, c] = x_ref[...]
    own(0)
    held[1, e, c] = dy_ref[...]
    for j in range(1, n):
        remote(
            w_ref, w_out.at[e], w_send.at[j], w_recv.at[j], expert=lax.rem(e + j, n)
        ).start()
    w_out[e] = w_ref[...]
    hop(0, 1)
    own(1)
    for k in range(2, n):
        hop(0, k)
    hop(1, 1)
    settle(0, x_out)
    for k in range(2, n):
        hop(1, k)
    settle(1, dy_out)
    for j in range(1, n):
        source = lax.rem(e + n - j, n)
        remote(
            w_ref, w_out.at[source], w_send.at[j], w_recv.at[j], expert=source
        ).wait()
    for a in range(2):
        pair(a, e, 0).wait_send()
        for direction in range(2):
            @pl.when(goes_on(direction))
            def _():
                line(a, direction, 0).wait_send()
            for k in range(1, n):
                @pl.when(arrives(direction, k))
                def _():
                    if k < n - 1:
                        @pl.when(goes_on(direction))
                        def _():
                            line(a, direction, k).wait_send()
                    pair(a, block(direction, k), direction * (n - 1) + k).wait_send()


def gather_rows(x, dy, w):
    n = lax.axis_size("expert")
    cores = lax.axis_size("tensor")
    rows, width = x.shape
    whole = jax.ShapeDtypeStruct((n * rows, cores * width), x.dtype)
    return pl.pallas_call(
        functools.partial(gather_kernel, n),
        out_shape=(whole, whole, jax.ShapeDtypeStruct((n,) + w.shape, w.dtype)),
        in_specs=[pl.BlockSpec(memory_space=pltpu.VMEM)] * 3,
        out_specs=[pl.BlockSpec(memory_space=pltpu.VMEM)] * 3,
        scratch_shapes=[
            pltpu.VMEM((2, n, cores, rows, width), x.dtype),
            pltpu.SemaphoreType.DMA((2, 2, n)),
            pltpu.SemaphoreType.DMA((2, 2, n)),
            pltpu.SemaphoreType.DMA((2, 2 * n)),
            pltpu.SemaphoreType.DMA((2, 2 * n)),
            pltpu.SemaphoreType.DMA((n,)),
            pltpu.SemaphoreType.DMA((n,)),
        ],
        compiler_params=pltpu.CompilerParams(
            collective_id=0, has_side_effects=True, vmem_limit_bytes=32 * 2**20
        ),
    )(x, dy, w)


def return_kernel(
    n, m, rows_ref, wide_ref, thin_ref, out_ref, wide_out, thin_out,
    from_up, from_down, summed, wide_in, thin_in,
    line_send, line_recv, peer_send, peer_recv,
):
    e = lax.axis_index("expert")
    d = lax.axis_index("dp")
    wide_type = jnp.float32
    barrier = pltpu.get_barrier_semaphore()
    for j in range(1, n):
        pl.semaphore_signal(
            barrier, inc=1, device_id={"expert": lax.rem(e + j, n)}, device_id_type=MESH
        )
    for j in range(1, m):
        pl.semaphore_signal(
            barrier, inc=1, device_id={"dp": lax.rem(d + j, m)}, device_id_type=MESH
        )
    pl.semaphore_wait(barrier, n + m - 2)

    landing = (from_up, from_down)

    def outgoing(direction, t, src):
        return remote(
            src, landing[direction].at[t], line_send.at[t], line_recv.at[direction, t],
            expert=e - 1 if direction == 0 else e + 1,
        )

    def incoming(direction, t):
        dst = landing[direction].at[t]
        return remote(
            dst, dst, line_send.at[t], line_recv.at[direction, t],
            expert=e + 1 if direction == 0 else e - 1,
        )

    def target(direction, step):
        return step - (n - 1) + e if direction == 0 else n - 1 - step + e

    def sends(direction, step):
        t = target(direction, step)
        if direction == 0:
            return jnp.logical_and(t >= 0, t < e)
        return jnp.logical_and(t <= n - 1, t > e)

    def starts_line(direction):
        return e == n - 1 if direction == 0 else e == 0

    def line_step(step):
        for direction in range(2):
            t = target(direction, step)
            go = sends(direction, step)

            @pl.when(jnp.logical_and(go, starts_line(direction)))
            def _():
                outgoing(direction, t, rows_ref.at[t]).start()

            @pl.when(jnp.logical_and(go, jnp.logical_not(starts_line(direction))))
            def _():
                incoming(direction, t).wait_recv()
                summed[t] = (
                    landing[direction][t].astype(wide_type) + rows_ref[t].astype(wide_type)
                ).astype(summed.dtype)
                outgoing(direction, t, summed.at[t]).start()

    line_step(0)
    pieces = ((wide_ref, wide_in), (thin_ref, thin_in))
    for j in range(1, m):
        for i, (src, dst) in enumerate(pieces):
            remote(
                src, dst.at[j - 1], peer_send.at[i, j], peer_recv.at[i, j], dp=lax.rem(d + j, m)
            ).start()
    for step in range(1, n - 1):
        line_step(step)
    for i, ((src, dst), out) in enumerate(zip(pieces, (wide_out, thin_out))):
        total = src[...].astype(wide_type)
        for j in range(1, m):
            remote(
                src, dst.at[j - 1], peer_send.at[i, j], peer_recv.at[i, j], dp=lax.rem(d + j, m)
            ).wait()
            total = total + dst[j - 1].astype(wide_type)
        out[...] = total

    @pl.when(e == 0)
    def _():
        incoming(0, e).wait_recv()
        out_ref[...] = (rows_ref[e].astype(wide_type) + from_up[e].astype(wide_type)).astype(
            out_ref.dtype
        )

    @pl.when(e == n - 1)
    def _():
        incoming(1, e).wait_recv()
        out_ref[...] = (rows_ref[e].astype(wide_type) + from_down[e].astype(wide_type)).astype(
            out_ref.dtype
        )

    @pl.when(jnp.logical_and(e > 0, e < n - 1))
    def _():
        incoming(0, e).wait_recv()
        incoming(1, e).wait_recv()
        out_ref[...] = (
            rows_ref[e].astype(wide_type)
            + from_up[e].astype(wide_type)
            + from_down[e].astype(wide_type)
        ).astype(out_ref.dtype)

    for step in range(n - 1):
        for direction in range(2):
            @pl.when(sends(direction, step))
            def _():
                t = target(direction, step)
                outgoing(direction, t, summed.at[t]).wait_send()


def return_rows(dx, wide, thin):
    n = lax.axis_size("expert")
    m = lax.axis_size("dp")
    shape = (n, dx.shape[0] // n, dx.shape[1])
    return pl.pallas_call(
        functools.partial(return_kernel, n, m),
        out_shape=(
            jax.ShapeDtypeStruct(shape[1:], dx.dtype),
            jax.ShapeDtypeStruct(wide.shape, jnp.float32),
            jax.ShapeDtypeStruct(thin.shape, jnp.float32),
        ),
        in_specs=[pl.BlockSpec(memory_space=pltpu.VMEM)] * 3,
        out_specs=[pl.BlockSpec(memory_space=pltpu.VMEM)] * 3,
        scratch_shapes=[
            pltpu.VMEM(shape, dx.dtype),
            pltpu.VMEM(shape, dx.dtype),
            pltpu.VMEM(shape, dx.dtype),
            pltpu.VMEM((m - 1,) + wide.shape, wide.dtype),
            pltpu.VMEM((m - 1,) + thin.shape, thin.dtype),
            pltpu.SemaphoreType.DMA((n,)),
            pltpu.SemaphoreType.DMA((2, n)),
            pltpu.SemaphoreType.DMA((2, m)),
            pltpu.SemaphoreType.DMA((2, m)),
        ],
        compiler_params=pltpu.CompilerParams(
            collective_id=1, has_side_effects=True, vmem_limit_bytes=32 * 2**20
        ),
    )(dx.reshape(shape), wide, thin)


def shards(
    activations,
    output_gradient,
    combine_weight,
    token_experts,
    gate_up_weight,
    gate_up_channel_scale,
    down_weight,
    down_channel_scale,
    adapter_input_first,
    adapter_input_second,
    adapter_down_first,
    adapter_down_second,
):
    single_float = jnp.float32
    brain_float_half = jnp.bfloat16
    n_expert = lax.axis_size("expert")
    local_count = gate_up_weight.shape[0]
    experts_all = local_count * n_expert
    tok_rows = activations.shape[0]
    top_count = token_experts.shape[1]
    capacity = min(tok_rows * top_count * 11 // (8 * experts_all), tok_rows)
    gradient_slice = activations.shape[1]
    slots_all = experts_all * capacity
    dense = (
        experts_all == top_count
        and capacity == tok_rows
        and local_count == 1
        and lax.axis_size("tensor") == 2
    )
    if dense:
        expert_ids = jnp.arange(experts_all, dtype=jnp.int32)
        token_weight = jnp.sum(
            jnp.where(
                token_experts[:, :, None] == expert_ids[None, None, :],
                combine_weight[:, :, None],
                0.0,
            ),
            axis=1,
        )
        spread = jnp.zeros((-(-experts_all // 8) * 8, tok_rows), jnp.float32)
        spread = lax.dynamic_update_slice(spread, token_weight.T, (0, 0))
        rows_x, rows_dy, weights = gather_rows(activations, output_gradient, spread)
        mine = lax.axis_index("expert")
        recv_w = lax.dynamic_slice_in_dim(weights, mine, 1, 1).reshape(1, -1)
        recv_x, recv_dy = rows_x[None], rows_dy[None]
    else:
        flat_experts = token_experts.reshape(tok_rows * top_count)
        onehot = (flat_experts[:, None] == jnp.arange(experts_all, dtype=jnp.int32)[None, :]).astype(
            jnp.int32
        )
        before = jnp.cumsum(onehot, axis=0, dtype=jnp.int32) - onehot
        counted = jnp.sum(before * onehot, axis=1, dtype=jnp.int32)
        slot_positions = jnp.where(counted < capacity, counted, -1).reshape(tok_rows, top_count)
        target = jnp.where(slot_positions >= 0, token_experts * capacity + slot_positions, -1)
        matched = target[None, :, :] == jnp.arange(slots_all, dtype=jnp.int32)[:, None, None]
        placing = jnp.any(matched, axis=2).astype(brain_float_half)
        slot_weight = jnp.sum(jnp.where(matched, combine_weight[None, :, :], 0.0), axis=(1, 2)).reshape(
            experts_all, capacity
        )
        whole_x, whole_dy = (
            lax.all_gather(activations, "tensor", axis=1, tiled=True),
            lax.all_gather(output_gradient, "tensor", axis=1, tiled=True),
        )
        d_whole = whole_x.shape[1]
        sent_x = (
            jnp.dot(placing, whole_x, preferred_element_type=single_float)
            .astype(brain_float_half)
            .reshape(experts_all, capacity, d_whole)
        )
        sent_dy = (
            jnp.dot(placing, whole_dy, preferred_element_type=single_float)
            .astype(brain_float_half)
            .reshape(experts_all, capacity, d_whole)
        )
        recv_x, recv_dy, recv_w = (
            lax.all_to_all(sent_x, "expert", split_axis=0, concat_axis=1, tiled=True),
            lax.all_to_all(sent_dy, "expert", split_axis=0, concat_axis=1, tiled=True),
            lax.all_to_all(
                slot_weight.astype(jnp.bfloat16), "expert", split_axis=0, concat_axis=1, tiled=True
            ).astype(slot_weight.dtype),
        )
    gradient_start = lax.axis_index("tensor") * gradient_slice
    gradient_listing = ([], [], [], [])
    input_rows = recv_x[0]
    dy_rows = recv_dy[0]
    gradient_rows = (recv_w[0][:, None] * dy_rows.astype(single_float)).astype(brain_float_half)
    scaled_gradient = (gradient_rows.astype(single_float) * down_channel_scale[0][None, :]).astype(
        brain_float_half
    )
    adapter_input_rows = jnp.dot(
        input_rows, adapter_input_first[0], preferred_element_type=single_float
    ).astype(brain_float_half)
    gate_values = (
        contract_product(input_rows, gate_up_weight[0, 0], 1, 1)
        * gate_up_channel_scale[0, 0][None, :]
    )
    gate_values = gate_values + ADAPTER_SCALE * jnp.dot(
        adapter_input_rows, adapter_input_second[0][:, 0, :], preferred_element_type=single_float
    )
    up_activation = (
        contract_product(input_rows, gate_up_weight[0, 1], 1, 1)
        * gate_up_channel_scale[0, 1][None, :]
    )
    up_activation = up_activation + ADAPTER_SCALE * jnp.dot(
        adapter_input_rows, adapter_input_second[0][:, 1, :], preferred_element_type=single_float
    )
    sig = jax.nn.sigmoid(ALPHA * gate_values)
    glu = gate_values * sig
    hidden_units = ((up_activation + 1.0) * glu).astype(brain_float_half)
    down_portion = jnp.dot(hidden_units, adapter_down_first[0], preferred_element_type=single_float)
    down_sum = lax.psum(down_portion.astype(jnp.bfloat16), "tensor").astype(jnp.float32)
    backward_adapter = contract_product(gradient_rows, adapter_down_second[0], 1, 1).astype(
        brain_float_half
    )
    hidden_gradient = contract_product(
        scaled_gradient, down_weight[0], 1, 1
    ) + ADAPTER_SCALE * contract_product(backward_adapter, adapter_down_first[0], 1, 1)
    d_up = hidden_gradient * glu
    d_gate = (
        hidden_gradient * (up_activation + 1.0) * sig * (1.0 + ALPHA * gate_values * (1.0 - sig))
    )
    d_both = jnp.stack([d_gate, d_up], axis=1)
    adapter_mid_gradient = d_both.astype(brain_float_half)
    dz_scaled = (d_both * gate_up_channel_scale[0][None, :, :]).astype(brain_float_half)
    input_portion = jnp.einsum(
        "ndy,tdy->nt",
        adapter_mid_gradient,
        adapter_input_second[0],
        preferred_element_type=single_float,
    )
    in_sum = lax.psum(input_portion.astype(jnp.bfloat16), "tensor").astype(jnp.float32)
    down_adapter = down_sum.astype(brain_float_half)
    input_adapter = in_sum.astype(brain_float_half)
    partial_value = jnp.einsum(
        "rjf,jfd->rd", dz_scaled, gate_up_weight[0], preferred_element_type=single_float
    )
    summed_values = lax.psum_scatter(
        partial_value.astype(jnp.bfloat16), "tensor", scatter_dimension=1, tiled=True
    ).astype(jnp.float32)
    input_first_rows = lax.dynamic_slice_in_dim(
        adapter_input_first[0], gradient_start, gradient_slice, 0
    )
    input_gradient_rows = (
        summed_values + ADAPTER_SCALE * contract_product(input_adapter, input_first_rows, 1, 1)
    ).astype(brain_float_half)
    dx_list = [input_gradient_rows]
    input_columns = lax.dynamic_slice_in_dim(input_rows, gradient_start, gradient_slice, 1)
    gradient_columns = lax.dynamic_slice_in_dim(gradient_rows, gradient_start, gradient_slice, 1)
    if dense:
        rank = input_adapter.shape[1]
        hidden_count = hidden_units.shape[1]
        wide = jnp.concatenate(
            [
                contract_product(input_adapter, input_columns, 0, 0),
                contract_product(down_adapter, gradient_columns, 0, 0),
            ],
            axis=0,
        )
        thin = jnp.concatenate(
            [
                contract_product(adapter_input_rows, adapter_mid_gradient[:, 0], 0, 0),
                contract_product(adapter_input_rows, adapter_mid_gradient[:, 1], 0, 0),
                contract_product(backward_adapter, hidden_units, 0, 0),
            ],
            axis=0,
        )
        input_grad, wide_sum, thin_sum = return_rows(
            dx_list[0],
            (ADAPTER_SCALE * wide).astype(brain_float_half),
            (ADAPTER_SCALE * thin).astype(brain_float_half),
        )
        return (
            input_grad,
            wide_sum[:rank].T[None],
            jnp.stack([thin_sum[:rank], thin_sum[rank : 2 * rank]], axis=1)[None],
            thin_sum[2 * rank :].T[None],
            wide_sum[rank:][None],
        )
    gradient_listing[0].append(ADAPTER_SCALE * contract_product(input_columns, input_adapter, 0, 0))
    gradient_listing[1].append(
        ADAPTER_SCALE
        * jnp.einsum(
            "hp,hwl->pwl",
            adapter_input_rows,
            adapter_mid_gradient,
            preferred_element_type=single_float,
        )
    )
    gradient_listing[2].append(
        ADAPTER_SCALE * contract_product(hidden_units, backward_adapter, 0, 0)
    )
    gradient_listing[3].append(
        ADAPTER_SCALE * contract_product(down_adapter, gradient_columns, 0, 0)
    )
    stacked = tuple((jnp.stack(items, axis=0) for items in gradient_listing))
    input_first_gradient, input_second_gradient, down_first_gradient, down_second_gradient = (
        lax.psum(stacked[0].astype(jnp.bfloat16), "dp").astype(jnp.float32),
        lax.psum(stacked[1].astype(jnp.bfloat16), "dp").astype(jnp.float32),
        lax.psum(stacked[2].astype(jnp.bfloat16), "dp").astype(jnp.float32),
        lax.psum(stacked[3].astype(jnp.bfloat16), "dp").astype(jnp.float32),
    )
    returned = lax.all_to_all(
        jnp.stack(dx_list, axis=0), "expert", split_axis=1, concat_axis=0, tiled=True
    )
    flat_rows = returned.reshape(slots_all, gradient_slice)
    input_grad = contract_product(placing, flat_rows, 0, 0).astype(brain_float_half)
    return (
        input_grad,
        input_first_gradient,
        input_second_gradient,
        down_first_gradient,
        down_second_gradient,
    )


def solution(mesh):
    placed = (
        P(("dp", "expert"), "tensor"),
        P(("dp", "expert"), "tensor"),
        P(("dp", "expert"), None),
        P(("dp", "expert"), None),
        P("expert", None, "tensor", None),
        P("expert", None, "tensor"),
        P("expert", "tensor", None),
        P("expert", None),
        P("expert", None, None),
        P("expert", None, None, "tensor"),
        P("expert", "tensor", None),
        P("expert", None, None),
    )
    return jax.shard_map(
        shards,
        mesh=mesh,
        in_specs=placed,
        out_specs=(
            P(("dp", "expert"), "tensor"),
            P("expert", "tensor", None),
            P("expert", None, None, "tensor"),
            P("expert", "tensor", None),
            P("expert", None, "tensor"),
        ),
        check_vma=False,
    )
```

```python
import functools

import jax
import jax.numpy as jnp
from jax import lax
from jax.experimental import pallas as pl
from jax.experimental.pallas import tpu as pltpu
from jax.sharding import PartitionSpec as P

ALPHA = 1.702
ADAPTER_SCALE = 2.0


def contract_product(left, right, left_dim, right_dim):
    return lax.dot_general(
        left, right, (((left_dim,), (right_dim,)), ((), ())), preferred_element_type=jnp.float32
    )


MESH = pl.DeviceIdType.MESH


def remote(src, dst, send, recv, **where):
    return pltpu.make_async_remote_copy(
        src_ref=src, dst_ref=dst, send_sem=send, recv_sem=recv, device_id=where, device_id_type=MESH
    )


def gather_kernel(
    n, x_ref, dy_ref, w_ref, x_out, dy_out, w_out,
    line_send, line_recv, pair_send, pair_recv, w_send, w_recv,
):
    e = lax.axis_index("expert")
    c = lax.axis_index("tensor")
    width, rows = x_ref.shape
    outs = (x_out, dy_out)
    barrier = pltpu.get_barrier_semaphore()
    for j in range(1, n):
        pl.semaphore_signal(
            barrier, inc=1, device_id={"expert": lax.rem(e + j, n)}, device_id_type=MESH
        )
    pl.semaphore_signal(barrier, inc=1, device_id={"tensor": 1 - c}, device_id_type=MESH)
    pl.semaphore_wait(barrier, n)

    def part(a, s, core):
        return outs[a].at[
            pl.ds(pl.multiple_of(core * width, width), width),
            pl.ds(pl.multiple_of(s * rows, rows), rows),
        ]

    def piece(a, s):
        return part(a, s, c)

    def block(direction, k):
        return e - k if direction == 0 else e + k

    def arrives(direction, k):
        return e >= k if direction == 0 else e + k <= n - 1

    def goes_on(direction):
        return e < n - 1 if direction == 0 else e > 0

    def line(a, direction, k):
        s = block(direction, k)
        return remote(
            piece(a, s), piece(a, s), line_send.at[a, direction, k], line_recv.at[a, direction, k],
            expert=e + 1 if direction == 0 else e - 1,
        )

    def line_in(a, direction, k):
        s = block(direction, k)
        return remote(
            piece(a, s), piece(a, s),
            line_send.at[a, direction, k - 1], line_recv.at[a, direction, k - 1],
            expert=e - 1 if direction == 0 else e + 1,
        )

    def pair(a, s, slot):
        return remote(
            piece(a, s), piece(a, s), pair_send.at[a, slot], pair_recv.at[a, slot], tensor=1 - c
        )

    def pair_in(a, s, slot):
        other = part(a, s, 1 - c)
        return remote(other, other, pair_send.at[a, slot], pair_recv.at[a, slot], tensor=1 - c)

    def own(a):
        for direction in range(2):
            @pl.when(goes_on(direction))
            def _():
                line(a, direction, 0).start()
        pair(a, e, 0).start()

    def hop(a, k):
        for direction in range(2):
            @pl.when(arrives(direction, k))
            def _():
                line_in(a, direction, k).wait_recv()
                if k < n - 1:
                    @pl.when(goes_on(direction))
                    def _():
                        line(a, direction, k).start()
                pair(a, block(direction, k), direction * (n - 1) + k).start()

    def settle(a):
        pair_in(a, e, 0).wait_recv()
        for k in range(1, n):
            for direction in range(2):
                @pl.when(arrives(direction, k))
                def _():
                    pair_in(a, block(direction, k), direction * (n - 1) + k).wait_recv()

    piece(0, e)[...] = x_ref[...]
    own(0)
    piece(1, e)[...] = dy_ref[...]
    for j in range(1, n):
        remote(
            w_ref, w_out.at[e], w_send.at[j], w_recv.at[j], expert=lax.rem(e + j, n)
        ).start()
    w_out[e] = w_ref[...]
    hop(0, 1)
    own(1)
    for k in range(2, n):
        hop(0, k)
    hop(1, 1)
    for k in range(2, n):
        hop(1, k)
    settle(0)
    settle(1)
    for j in range(1, n):
        source = lax.rem(e + n - j, n)
        remote(
            w_ref, w_out.at[source], w_send.at[j], w_recv.at[j], expert=source
        ).wait()
    for a in range(2):
        pair(a, e, 0).wait_send()
        for direction in range(2):
            @pl.when(goes_on(direction))
            def _():
                line(a, direction, 0).wait_send()
            for k in range(1, n):
                @pl.when(arrives(direction, k))
                def _():
                    if k < n - 1:
                        @pl.when(goes_on(direction))
                        def _():
                            line(a, direction, k).wait_send()
                    pair(a, block(direction, k), direction * (n - 1) + k).wait_send()


def gather_rows(x, dy, w):
    n = lax.axis_size("expert")
    cores = lax.axis_size("tensor")
    width, rows = x.shape
    whole = jax.ShapeDtypeStruct((cores * width, n * rows), x.dtype)
    return pl.pallas_call(
        functools.partial(gather_kernel, n),
        out_shape=(whole, whole, jax.ShapeDtypeStruct((n,) + w.shape, w.dtype)),
        in_specs=[pl.BlockSpec(memory_space=pltpu.VMEM)] * 3,
        out_specs=[pl.BlockSpec(memory_space=pltpu.VMEM)] * 3,
        scratch_shapes=[
            pltpu.SemaphoreType.DMA((2, 2, n)),
            pltpu.SemaphoreType.DMA((2, 2, n)),
            pltpu.SemaphoreType.DMA((2, 2 * n)),
            pltpu.SemaphoreType.DMA((2, 2 * n)),
            pltpu.SemaphoreType.DMA((n,)),
            pltpu.SemaphoreType.DMA((n,)),
        ],
        compiler_params=pltpu.CompilerParams(
            collective_id=0, has_side_effects=True, vmem_limit_bytes=32 * 2**20
        ),
    )(x, dy, w)


def return_kernel(
    n, m, part_ref, wide_ref, thin_ref, out_ref, wide_out, thin_out,
    from_up, from_down, summed, wide_in, thin_in, rows_ref, other_in,
    line_send, line_recv, peer_send, peer_recv, pair_send, pair_recv,
):
    e = lax.axis_index("expert")
    c = lax.axis_index("tensor")
    d = lax.axis_index("dp")
    wide_type = jnp.float32
    barrier = pltpu.get_barrier_semaphore()
    for j in range(1, n):
        pl.semaphore_signal(
            barrier, inc=1, device_id={"expert": lax.rem(e + j, n)}, device_id_type=MESH
        )
    for j in range(1, m):
        pl.semaphore_signal(
            barrier, inc=1, device_id={"dp": lax.rem(d + j, m)}, device_id_type=MESH
        )
    pl.semaphore_signal(barrier, inc=1, device_id={"tensor": 1 - c}, device_id_type=MESH)
    half, rows = out_ref.shape

    order = tuple(t for i in range((n + 1) // 2) for t in dict.fromkeys((i, n - 1 - i)))

    def part(t, core):
        return part_ref.at[
            pl.ds(pl.multiple_of(core * half, half), half), pl.ds(t * rows, rows)
        ]

    def exchange(t):
        return remote(
            part(t, 1 - c), other_in.at[t], pair_send.at[t], pair_recv.at[t], tensor=1 - c
        )

    pl.semaphore_wait(barrier, n + m - 1)
    for t in order:
        exchange(t).start()

    def join(t):
        exchange(t).wait_recv()
        rows_ref[t] = (part(t, c)[...].astype(wide_type) + other_in[t].astype(wide_type)).astype(
            rows_ref.dtype
        )

    landing = (from_up, from_down)

    def outgoing(direction, t, src):
        return remote(
            src, landing[direction].at[t], line_send.at[t], line_recv.at[direction, t],
            expert=e - 1 if direction == 0 else e + 1,
        )

    def incoming(direction, t):
        dst = landing[direction].at[t]
        return remote(
            dst, dst, line_send.at[t], line_recv.at[direction, t],
            expert=e + 1 if direction == 0 else e - 1,
        )

    def target(direction, step):
        return step - (n - 1) + e if direction == 0 else n - 1 - step + e

    def sends(direction, step):
        t = target(direction, step)
        if direction == 0:
            return jnp.logical_and(t >= 0, t < e)
        return jnp.logical_and(t <= n - 1, t > e)

    def starts_line(direction):
        return e == n - 1 if direction == 0 else e == 0

    def line_step(step):
        for direction in range(2):
            t = target(direction, step)
            go = sends(direction, step)

            @pl.when(jnp.logical_and(go, starts_line(direction)))
            def _():
                outgoing(direction, t, rows_ref.at[t]).start()

            @pl.when(jnp.logical_and(go, jnp.logical_not(starts_line(direction))))
            def _():
                incoming(direction, t).wait_recv()
                summed[t] = (
                    landing[direction][t].astype(wide_type) + rows_ref[t].astype(wide_type)
                ).astype(summed.dtype)
                outgoing(direction, t, summed.at[t]).start()

    for t in order[:2]:
        join(t)
    line_step(0)
    for t in order[2:]:
        join(t)
    pieces = ((wide_ref, wide_in), (thin_ref, thin_in))
    for j in range(1, m):
        for i, (src, dst) in enumerate(pieces):
            remote(
                src, dst.at[j - 1], peer_send.at[i, j], peer_recv.at[i, j], dp=lax.rem(d + j, m)
            ).start()
    for step in range(1, n - 1):
        line_step(step)
    for i, ((src, dst), out) in enumerate(zip(pieces, (wide_out, thin_out))):
        total = src[...].astype(wide_type)
        for j in range(1, m):
            remote(
                src, dst.at[j - 1], peer_send.at[i, j], peer_recv.at[i, j], dp=lax.rem(d + j, m)
            ).wait()
            total = total + dst[j - 1].astype(wide_type)
        out[...] = total

    @pl.when(e == 0)
    def _():
        incoming(0, e).wait_recv()
        out_ref[...] = (rows_ref[e].astype(wide_type) + from_up[e].astype(wide_type)).astype(
            out_ref.dtype
        )

    @pl.when(e == n - 1)
    def _():
        incoming(1, e).wait_recv()
        out_ref[...] = (rows_ref[e].astype(wide_type) + from_down[e].astype(wide_type)).astype(
            out_ref.dtype
        )

    @pl.when(jnp.logical_and(e > 0, e < n - 1))
    def _():
        incoming(0, e).wait_recv()
        incoming(1, e).wait_recv()
        out_ref[...] = (
            rows_ref[e].astype(wide_type)
            + from_up[e].astype(wide_type)
            + from_down[e].astype(wide_type)
        ).astype(out_ref.dtype)

    for t in order:
        exchange(t).wait_send()
    for step in range(n - 1):
        for direction in range(2):
            @pl.when(sends(direction, step))
            def _():
                t = target(direction, step)
                outgoing(direction, t, summed.at[t]).wait_send()


def return_rows(dx, wide, thin):
    n = lax.axis_size("expert")
    m = lax.axis_size("dp")
    cores = lax.axis_size("tensor")
    shape = (n, dx.shape[0] // cores, dx.shape[1] // n)
    return pl.pallas_call(
        functools.partial(return_kernel, n, m),
        out_shape=(
            jax.ShapeDtypeStruct(shape[1:], dx.dtype),
            jax.ShapeDtypeStruct(wide.shape, jnp.float32),
            jax.ShapeDtypeStruct(thin.shape, jnp.float32),
        ),
        in_specs=[pl.BlockSpec(memory_space=pltpu.VMEM)] * 3,
        out_specs=[pl.BlockSpec(memory_space=pltpu.VMEM)] * 3,
        scratch_shapes=[
            pltpu.VMEM(shape, dx.dtype),
            pltpu.VMEM(shape, dx.dtype),
            pltpu.VMEM(shape, dx.dtype),
            pltpu.VMEM((m - 1,) + wide.shape, wide.dtype),
            pltpu.VMEM((m - 1,) + thin.shape, thin.dtype),
            pltpu.VMEM(shape, dx.dtype),
            pltpu.VMEM(shape, dx.dtype),
            pltpu.SemaphoreType.DMA((n,)),
            pltpu.SemaphoreType.DMA((2, n)),
            pltpu.SemaphoreType.DMA((2, m)),
            pltpu.SemaphoreType.DMA((2, m)),
            pltpu.SemaphoreType.DMA((n,)),
            pltpu.SemaphoreType.DMA((n,)),
        ],
        compiler_params=pltpu.CompilerParams(
            collective_id=1, has_side_effects=True, vmem_limit_bytes=32 * 2**20
        ),
    )(dx, wide, thin)


def shards(
    activations,
    output_gradient,
    combine_weight,
    token_experts,
    gate_up_weight,
    gate_up_channel_scale,
    down_weight,
    down_channel_scale,
    adapter_input_first,
    adapter_input_second,
    adapter_down_first,
    adapter_down_second,
):
    single_float = jnp.float32
    brain_float_half = jnp.bfloat16
    n_expert = lax.axis_size("expert")
    local_count = gate_up_weight.shape[0]
    experts_all = local_count * n_expert
    tok_rows = activations.shape[0]
    top_count = token_experts.shape[1]
    capacity = min(tok_rows * top_count * 11 // (8 * experts_all), tok_rows)
    gradient_slice = activations.shape[1]
    slots_all = experts_all * capacity
    dense = (
        experts_all == top_count
        and capacity == tok_rows
        and local_count == 1
        and lax.axis_size("tensor") == 2
        and tok_rows % 128 == 0
        and gradient_slice % 16 == 0
    )
    if dense:
        expert_ids = jnp.arange(experts_all, dtype=jnp.int32)
        token_weight = jnp.sum(
            jnp.where(
                token_experts[:, :, None] == expert_ids[None, None, :],
                combine_weight[:, :, None],
                0.0,
            ),
            axis=1,
        )
        spread = jnp.zeros((-(-experts_all // 8) * 8, tok_rows), jnp.float32)
        spread = lax.dynamic_update_slice(spread, token_weight.T, (0, 0))
        rows_x, rows_dy, weights = gather_rows(
            activations.T, output_gradient.T, spread
        )
        mine = lax.axis_index("expert")
        recv_w = lax.dynamic_slice_in_dim(weights, mine, 1, 1).reshape(1, -1)
        recv_x, recv_dy = rows_x.T[None], rows_dy.T[None]
    else:
        flat_experts = token_experts.reshape(tok_rows * top_count)
        onehot = (flat_experts[:, None] == jnp.arange(experts_all, dtype=jnp.int32)[None, :]).astype(
            jnp.int32
        )
        before = jnp.cumsum(onehot, axis=0, dtype=jnp.int32) - onehot
        counted = jnp.sum(before * onehot, axis=1, dtype=jnp.int32)
        slot_positions = jnp.where(counted < capacity, counted, -1).reshape(tok_rows, top_count)
        target = jnp.where(slot_positions >= 0, token_experts * capacity + slot_positions, -1)
        matched = target[None, :, :] == jnp.arange(slots_all, dtype=jnp.int32)[:, None, None]
        placing = jnp.any(matched, axis=2).astype(brain_float_half)
        slot_weight = jnp.sum(jnp.where(matched, combine_weight[None, :, :], 0.0), axis=(1, 2)).reshape(
            experts_all, capacity
        )
        whole_x, whole_dy = (
            lax.all_gather(activations, "tensor", axis=1, tiled=True),
            lax.all_gather(output_gradient, "tensor", axis=1, tiled=True),
        )
        d_whole = whole_x.shape[1]
        sent_x = (
            jnp.dot(placing, whole_x, preferred_element_type=single_float)
            .astype(brain_float_half)
            .reshape(experts_all, capacity, d_whole)
        )
        sent_dy = (
            jnp.dot(placing, whole_dy, preferred_element_type=single_float)
            .astype(brain_float_half)
            .reshape(experts_all, capacity, d_whole)
        )
        recv_x, recv_dy, recv_w = (
            lax.all_to_all(sent_x, "expert", split_axis=0, concat_axis=1, tiled=True),
            lax.all_to_all(sent_dy, "expert", split_axis=0, concat_axis=1, tiled=True),
            lax.all_to_all(
                slot_weight.astype(jnp.bfloat16), "expert", split_axis=0, concat_axis=1, tiled=True
            ).astype(slot_weight.dtype),
        )
    gradient_start = lax.axis_index("tensor") * gradient_slice
    gradient_listing = ([], [], [], [])
    input_rows = recv_x[0]
    dy_rows = recv_dy[0]
    gradient_rows = (recv_w[0][:, None] * dy_rows.astype(single_float)).astype(brain_float_half)
    scaled_gradient = (gradient_rows.astype(single_float) * down_channel_scale[0][None, :]).astype(
        brain_float_half
    )
    adapter_input_rows = jnp.dot(
        input_rows, adapter_input_first[0], preferred_element_type=single_float
    ).astype(brain_float_half)
    gate_values = (
        contract_product(input_rows, gate_up_weight[0, 0], 1, 1)
        * gate_up_channel_scale[0, 0][None, :]
    )
    gate_values = gate_values + ADAPTER_SCALE * jnp.dot(
        adapter_input_rows, adapter_input_second[0][:, 0, :], preferred_element_type=single_float
    )
    up_activation = (
        contract_product(input_rows, gate_up_weight[0, 1], 1, 1)
        * gate_up_channel_scale[0, 1][None, :]
    )
    up_activation = up_activation + ADAPTER_SCALE * jnp.dot(
        adapter_input_rows, adapter_input_second[0][:, 1, :], preferred_element_type=single_float
    )
    sig = jax.nn.sigmoid(ALPHA * gate_values)
    glu = gate_values * sig
    hidden_units = ((up_activation + 1.0) * glu).astype(brain_float_half)
    down_portion = jnp.dot(hidden_units, adapter_down_first[0], preferred_element_type=single_float)
    down_sum = lax.psum(down_portion.astype(jnp.bfloat16), "tensor").astype(jnp.float32)
    backward_adapter = contract_product(gradient_rows, adapter_down_second[0], 1, 1).astype(
        brain_float_half
    )
    hidden_gradient = contract_product(
        scaled_gradient, down_weight[0], 1, 1
    ) + ADAPTER_SCALE * contract_product(backward_adapter, adapter_down_first[0], 1, 1)
    d_up = hidden_gradient * glu
    d_gate = (
        hidden_gradient * (up_activation + 1.0) * sig * (1.0 + ALPHA * gate_values * (1.0 - sig))
    )
    d_both = jnp.stack([d_gate, d_up], axis=1)
    adapter_mid_gradient = d_both.astype(brain_float_half)
    dz_scaled = (d_both * gate_up_channel_scale[0][None, :, :]).astype(brain_float_half)
    input_portion = jnp.einsum(
        "ndy,tdy->nt",
        adapter_mid_gradient,
        adapter_input_second[0],
        preferred_element_type=single_float,
    )
    in_sum = lax.psum(input_portion.astype(jnp.bfloat16), "tensor").astype(jnp.float32)
    down_adapter = down_sum.astype(brain_float_half)
    input_adapter = in_sum.astype(brain_float_half)
    partial_value = jnp.einsum(
        "rjf,jfd->rd", dz_scaled, gate_up_weight[0], preferred_element_type=single_float
    )
    if dense:
        partial_rows = (
            partial_value
            + ADAPTER_SCALE
            * contract_product(input_portion.astype(brain_float_half), adapter_input_first[0], 1, 1)
        ).astype(brain_float_half)
    else:
        summed_values = lax.psum_scatter(
            partial_value.astype(jnp.bfloat16), "tensor", scatter_dimension=1, tiled=True
        ).astype(jnp.float32)
        input_first_rows = lax.dynamic_slice_in_dim(
            adapter_input_first[0], gradient_start, gradient_slice, 0
        )
        input_gradient_rows = (
            summed_values + ADAPTER_SCALE * contract_product(input_adapter, input_first_rows, 1, 1)
        ).astype(brain_float_half)
        dx_list = [input_gradient_rows]
    input_columns = lax.dynamic_slice_in_dim(input_rows, gradient_start, gradient_slice, 1)
    gradient_columns = lax.dynamic_slice_in_dim(gradient_rows, gradient_start, gradient_slice, 1)
    if dense:
        rank = input_adapter.shape[1]
        hidden_count = hidden_units.shape[1]
        wide = jnp.concatenate(
            [
                contract_product(input_adapter, input_columns, 0, 0),
                contract_product(down_adapter, gradient_columns, 0, 0),
            ],
            axis=0,
        )
        thin = jnp.concatenate(
            [
                contract_product(adapter_input_rows, adapter_mid_gradient[:, 0], 0, 0),
                contract_product(adapter_input_rows, adapter_mid_gradient[:, 1], 0, 0),
                contract_product(backward_adapter, hidden_units, 0, 0),
            ],
            axis=0,
        )
        input_grad, wide_sum, thin_sum = return_rows(
            partial_rows.T,
            (ADAPTER_SCALE * wide).astype(brain_float_half),
            (ADAPTER_SCALE * thin).astype(brain_float_half),
        )
        return (
            input_grad.T,
            wide_sum[:rank].T[None],
            jnp.stack([thin_sum[:rank], thin_sum[rank : 2 * rank]], axis=1)[None],
            thin_sum[2 * rank :].T[None],
            wide_sum[rank:][None],
        )
    gradient_listing[0].append(ADAPTER_SCALE * contract_product(input_columns, input_adapter, 0, 0))
    gradient_listing[1].append(
        ADAPTER_SCALE
        * jnp.einsum(
            "hp,hwl->pwl",
            adapter_input_rows,
            adapter_mid_gradient,
            preferred_element_type=single_float,
        )
    )
    gradient_listing[2].append(
        ADAPTER_SCALE * contract_product(hidden_units, backward_adapter, 0, 0)
    )
    gradient_listing[3].append(
        ADAPTER_SCALE * contract_product(down_adapter, gradient_columns, 0, 0)
    )
    stacked = tuple((jnp.stack(items, axis=0) for items in gradient_listing))
    input_first_gradient, input_second_gradient, down_first_gradient, down_second_gradient = (
        lax.psum(stacked[0].astype(jnp.bfloat16), "dp").astype(jnp.float32),
        lax.psum(stacked[1].astype(jnp.bfloat16), "dp").astype(jnp.float32),
        lax.psum(stacked[2].astype(jnp.bfloat16), "dp").astype(jnp.float32),
        lax.psum(stacked[3].astype(jnp.bfloat16), "dp").astype(jnp.float32),
    )
    returned = lax.all_to_all(
        jnp.stack(dx_list, axis=0), "expert", split_axis=1, concat_axis=0, tiled=True
    )
    flat_rows = returned.reshape(slots_all, gradient_slice)
    input_grad = contract_product(placing, flat_rows, 0, 0).astype(brain_float_half)
    return (
        input_grad,
        input_first_gradient,
        input_second_gradient,
        down_first_gradient,
        down_second_gradient,
    )


def solution(mesh):
    placed = (
        P(("dp", "expert"), "tensor"),
        P(("dp", "expert"), "tensor"),
        P(("dp", "expert"), None),
        P(("dp", "expert"), None),
        P("expert", None, "tensor", None),
        P("expert", None, "tensor"),
        P("expert", "tensor", None),
        P("expert", None),
        P("expert", None, None),
        P("expert", None, None, "tensor"),
        P("expert", "tensor", None),
        P("expert", None, None),
    )
    return jax.shard_map(
        shards,
        mesh=mesh,
        in_specs=placed,
        out_specs=(
            P(("dp", "expert"), "tensor"),
            P("expert", "tensor", None),
            P("expert", None, None, "tensor"),
            P("expert", "tensor", None),
            P("expert", None, "tensor"),
        ),
        check_vma=False,
    )
```

```python
import functools

import jax
import jax.numpy as jnp
from jax import lax
from jax.experimental import pallas as pl
from jax.experimental.pallas import tpu as pltpu
from jax.sharding import PartitionSpec as P

ALPHA = 1.702
ADAPTER_SCALE = 2.0


def contract_product(left, right, left_dim, right_dim):
    return lax.dot_general(
        left, right, (((left_dim,), (right_dim,)), ((), ())), preferred_element_type=jnp.float32
    )


MESH = pl.DeviceIdType.MESH


def remote(src, dst, send, recv, **where):
    return pltpu.make_async_remote_copy(
        src_ref=src, dst_ref=dst, send_sem=send, recv_sem=recv, device_id=where, device_id_type=MESH
    )


def gather_kernel(
    n, x_ref, dy_ref, w_ref, x_out, dy_out, w_out,
    line_send, line_recv, pair_send, pair_recv, w_send, w_recv,
):
    e = lax.axis_index("expert")
    c = lax.axis_index("tensor")
    width, rows = x_ref.shape
    outs = (x_out, dy_out)
    barrier = pltpu.get_barrier_semaphore()
    for j in range(1, n):
        pl.semaphore_signal(
            barrier, inc=1, device_id={"expert": lax.rem(e + j, n)}, device_id_type=MESH
        )
    pl.semaphore_signal(barrier, inc=1, device_id={"tensor": 1 - c}, device_id_type=MESH)
    pl.semaphore_wait(barrier, n)

    def part(a, s, core):
        return outs[a].at[
            pl.ds(pl.multiple_of(core * width, width), width),
            pl.ds(pl.multiple_of(s * rows, rows), rows),
        ]

    def piece(a, s):
        return part(a, s, c)

    def block(direction, k):
        return e - k if direction == 0 else e + k

    def arrives(direction, k):
        return e >= k if direction == 0 else e + k <= n - 1

    def goes_on(direction):
        return e < n - 1 if direction == 0 else e > 0

    def line(a, direction, k):
        s = block(direction, k)
        return remote(
            piece(a, s), piece(a, s), line_send.at[a, direction, k], line_recv.at[a, direction, k],
            expert=e + 1 if direction == 0 else e - 1,
        )

    def line_in(a, direction, k):
        s = block(direction, k)
        return remote(
            piece(a, s), piece(a, s),
            line_send.at[a, direction, k - 1], line_recv.at[a, direction, k - 1],
            expert=e - 1 if direction == 0 else e + 1,
        )

    def pair(a, s, slot):
        return remote(
            piece(a, s), piece(a, s), pair_send.at[a, slot], pair_recv.at[a, slot], tensor=1 - c
        )

    def pair_in(a, s, slot):
        other = part(a, s, 1 - c)
        return remote(other, other, pair_send.at[a, slot], pair_recv.at[a, slot], tensor=1 - c)

    def own(a):
        for direction in range(2):
            @pl.when(goes_on(direction))
            def _():
                line(a, direction, 0).start()
        pair(a, e, 0).start()

    def hop(a, k):
        for direction in range(2):
            @pl.when(arrives(direction, k))
            def _():
                line_in(a, direction, k).wait_recv()
                if k < n - 1:
                    @pl.when(goes_on(direction))
                    def _():
                        line(a, direction, k).start()
                pair(a, block(direction, k), direction * (n - 1) + k).start()

    def settle(a):
        pair_in(a, e, 0).wait_recv()
        for k in range(1, n):
            for direction in range(2):
                @pl.when(arrives(direction, k))
                def _():
                    pair_in(a, block(direction, k), direction * (n - 1) + k).wait_recv()

    piece(0, e)[...] = x_ref[...]
    own(0)
    piece(1, e)[...] = dy_ref[...]
    for j in range(1, n):
        remote(
            w_ref, w_out.at[e], w_send.at[j], w_recv.at[j], expert=lax.rem(e + j, n)
        ).start()
    w_out[e] = w_ref[...]
    hop(0, 1)
    own(1)
    for k in range(2, n):
        hop(0, k)
    hop(1, 1)
    for k in range(2, n):
        hop(1, k)
    settle(0)
    settle(1)
    for j in range(1, n):
        source = lax.rem(e + n - j, n)
        remote(
            w_ref, w_out.at[source], w_send.at[j], w_recv.at[j], expert=source
        ).wait()
    for a in range(2):
        pair(a, e, 0).wait_send()
        for direction in range(2):
            @pl.when(goes_on(direction))
            def _():
                line(a, direction, 0).wait_send()
            for k in range(1, n):
                @pl.when(arrives(direction, k))
                def _():
                    if k < n - 1:
                        @pl.when(goes_on(direction))
                        def _():
                            line(a, direction, k).wait_send()
                    pair(a, block(direction, k), direction * (n - 1) + k).wait_send()


def gather_rows(x, dy, w):
    n = lax.axis_size("expert")
    cores = lax.axis_size("tensor")
    width, rows = x.shape
    whole = jax.ShapeDtypeStruct((cores * width, n * rows), x.dtype)
    return pl.pallas_call(
        functools.partial(gather_kernel, n),
        out_shape=(whole, whole, jax.ShapeDtypeStruct((n,) + w.shape, w.dtype)),
        in_specs=[pl.BlockSpec(memory_space=pltpu.VMEM)] * 3,
        out_specs=[pl.BlockSpec(memory_space=pltpu.VMEM)] * 3,
        scratch_shapes=[
            pltpu.SemaphoreType.DMA((2, 2, n)),
            pltpu.SemaphoreType.DMA((2, 2, n)),
            pltpu.SemaphoreType.DMA((2, 2 * n)),
            pltpu.SemaphoreType.DMA((2, 2 * n)),
            pltpu.SemaphoreType.DMA((n,)),
            pltpu.SemaphoreType.DMA((n,)),
        ],
        compiler_params=pltpu.CompilerParams(
            collective_id=0, has_side_effects=True, vmem_limit_bytes=32 * 2**20
        ),
    )(x, dy, w)


def return_kernel(
    n, m, part_ref, wide_ref, thin_ref, out_ref, wide_out, thin_out,
    from_up, from_down, summed, wide_in, thin_in, rows_ref, other_in,
    line_send, line_recv, peer_send, peer_recv, pair_send, pair_recv,
):
    e = lax.axis_index("expert")
    c = lax.axis_index("tensor")
    d = lax.axis_index("dp")
    wide_type = jnp.float32
    barrier = pltpu.get_barrier_semaphore()
    for j in range(1, n):
        pl.semaphore_signal(
            barrier, inc=1, device_id={"expert": lax.rem(e + j, n)}, device_id_type=MESH
        )
    for j in range(1, m):
        pl.semaphore_signal(
            barrier, inc=1, device_id={"dp": lax.rem(d + j, m)}, device_id_type=MESH
        )
    pl.semaphore_signal(barrier, inc=1, device_id={"tensor": 1 - c}, device_id_type=MESH)
    half, rows = out_ref.shape

    order = tuple(t for i in range((n + 1) // 2) for t in dict.fromkeys((i, n - 1 - i)))

    def part(t, core):
        return part_ref.at[
            pl.ds(pl.multiple_of(core * half, half), half), pl.ds(t * rows, rows)
        ]

    def exchange(t):
        return remote(
            part(t, 1 - c), other_in.at[t], pair_send.at[t], pair_recv.at[t], tensor=1 - c
        )

    pl.semaphore_wait(barrier, n + m - 1)
    for t in order:
        exchange(t).start()

    def join(t):
        exchange(t).wait_recv()
        rows_ref[t] = (part(t, c)[...].astype(wide_type) + other_in[t].astype(wide_type)).astype(
            rows_ref.dtype
        )

    landing = (from_up, from_down)

    def outgoing(direction, t, src):
        return remote(
            src, landing[direction].at[t], line_send.at[t], line_recv.at[direction, t],
            expert=e - 1 if direction == 0 else e + 1,
        )

    def incoming(direction, t):
        dst = landing[direction].at[t]
        return remote(
            dst, dst, line_send.at[t], line_recv.at[direction, t],
            expert=e + 1 if direction == 0 else e - 1,
        )

    def target(direction, step):
        return step - (n - 1) + e if direction == 0 else n - 1 - step + e

    def sends(direction, step):
        t = target(direction, step)
        if direction == 0:
            return jnp.logical_and(t >= 0, t < e)
        return jnp.logical_and(t <= n - 1, t > e)

    def starts_line(direction):
        return e == n - 1 if direction == 0 else e == 0

    def line_step(step):
        for direction in range(2):
            t = target(direction, step)
            go = sends(direction, step)

            @pl.when(jnp.logical_and(go, starts_line(direction)))
            def _():
                outgoing(direction, t, rows_ref.at[t]).start()

            @pl.when(jnp.logical_and(go, jnp.logical_not(starts_line(direction))))
            def _():
                incoming(direction, t).wait_recv()
                summed[t] = (
                    landing[direction][t].astype(wide_type) + rows_ref[t].astype(wide_type)
                ).astype(summed.dtype)
                outgoing(direction, t, summed.at[t]).start()

    for t in order[:2]:
        join(t)
    line_step(0)
    for t in order[2:]:
        join(t)
    pieces = ((wide_ref, wide_in), (thin_ref, thin_in))
    for j in range(1, m):
        for i, (src, dst) in enumerate(pieces):
            remote(
                src, dst.at[j - 1], peer_send.at[i, j], peer_recv.at[i, j], dp=lax.rem(d + j, m)
            ).start()
    for step in range(1, n - 1):
        line_step(step)
    for i, ((src, dst), out) in enumerate(zip(pieces, (wide_out, thin_out))):
        total = src[...].astype(wide_type)
        for j in range(1, m):
            remote(
                src, dst.at[j - 1], peer_send.at[i, j], peer_recv.at[i, j], dp=lax.rem(d + j, m)
            ).wait()
            total = total + dst[j - 1].astype(wide_type)
        out[...] = total

    @pl.when(e == 0)
    def _():
        incoming(0, e).wait_recv()
        out_ref[...] = (rows_ref[e].astype(wide_type) + from_up[e].astype(wide_type)).astype(
            out_ref.dtype
        )

    @pl.when(e == n - 1)
    def _():
        incoming(1, e).wait_recv()
        out_ref[...] = (rows_ref[e].astype(wide_type) + from_down[e].astype(wide_type)).astype(
            out_ref.dtype
        )

    @pl.when(jnp.logical_and(e > 0, e < n - 1))
    def _():
        incoming(0, e).wait_recv()
        incoming(1, e).wait_recv()
        out_ref[...] = (
            rows_ref[e].astype(wide_type)
            + from_up[e].astype(wide_type)
            + from_down[e].astype(wide_type)
        ).astype(out_ref.dtype)

    for t in order:
        exchange(t).wait_send()
    for step in range(n - 1):
        for direction in range(2):
            @pl.when(sends(direction, step))
            def _():
                t = target(direction, step)
                outgoing(direction, t, summed.at[t]).wait_send()


def return_rows(dx, wide, thin):
    n = lax.axis_size("expert")
    m = lax.axis_size("dp")
    cores = lax.axis_size("tensor")
    shape = (n, dx.shape[0] // cores, dx.shape[1] // n)
    return pl.pallas_call(
        functools.partial(return_kernel, n, m),
        out_shape=(
            jax.ShapeDtypeStruct(shape[1:], dx.dtype),
            jax.ShapeDtypeStruct(wide.shape, jnp.float32),
            jax.ShapeDtypeStruct(thin.shape, jnp.float32),
        ),
        in_specs=[pl.BlockSpec(memory_space=pltpu.VMEM)] * 3,
        out_specs=[pl.BlockSpec(memory_space=pltpu.VMEM)] * 3,
        scratch_shapes=[
            pltpu.VMEM(shape, dx.dtype),
            pltpu.VMEM(shape, dx.dtype),
            pltpu.VMEM(shape, dx.dtype),
            pltpu.VMEM((m - 1,) + wide.shape, wide.dtype),
            pltpu.VMEM((m - 1,) + thin.shape, thin.dtype),
            pltpu.VMEM(shape, dx.dtype),
            pltpu.VMEM(shape, dx.dtype),
            pltpu.SemaphoreType.DMA((n,)),
            pltpu.SemaphoreType.DMA((2, n)),
            pltpu.SemaphoreType.DMA((2, m)),
            pltpu.SemaphoreType.DMA((2, m)),
            pltpu.SemaphoreType.DMA((n,)),
            pltpu.SemaphoreType.DMA((n,)),
        ],
        compiler_params=pltpu.CompilerParams(
            collective_id=1, has_side_effects=True, vmem_limit_bytes=32 * 2**20
        ),
    )(dx, wide, thin)


def shards(
    activations,
    output_gradient,
    combine_weight,
    token_experts,
    gate_up_weight,
    gate_up_channel_scale,
    down_weight,
    down_channel_scale,
    adapter_input_first,
    adapter_input_second,
    adapter_down_first,
    adapter_down_second,
):
    single_float = jnp.float32
    brain_float_half = jnp.bfloat16
    n_expert = lax.axis_size("expert")
    local_count = gate_up_weight.shape[0]
    experts_all = local_count * n_expert
    tok_rows = activations.shape[0]
    top_count = token_experts.shape[1]
    capacity = min(tok_rows * top_count * 11 // (8 * experts_all), tok_rows)
    gradient_slice = activations.shape[1]
    slots_all = experts_all * capacity
    dense = (
        experts_all == top_count
        and capacity == tok_rows
        and local_count == 1
        and lax.axis_size("tensor") == 2
        and tok_rows % 128 == 0
        and gradient_slice % 16 == 0
    )
    if dense:
        expert_ids = jnp.arange(experts_all, dtype=jnp.int32)
        token_weight = jnp.sum(
            jnp.where(
                token_experts[:, :, None] == expert_ids[None, None, :],
                combine_weight[:, :, None],
                0.0,
            ),
            axis=1,
        )
        spread = jnp.zeros((-(-experts_all // 8) * 8, tok_rows), jnp.float32)
        spread = lax.dynamic_update_slice(spread, token_weight.T, (0, 0))
        rows_x, rows_dy, weights = gather_rows(
            activations.T, output_gradient.T, spread
        )
        mine = lax.axis_index("expert")
        recv_w = lax.dynamic_slice_in_dim(weights, mine, 1, 1).reshape(1, -1)
        recv_x, recv_dy = rows_x.T[None], rows_dy.T[None]
    else:
        flat_experts = token_experts.reshape(tok_rows * top_count)
        onehot = (flat_experts[:, None] == jnp.arange(experts_all, dtype=jnp.int32)[None, :]).astype(
            jnp.int32
        )
        before = jnp.cumsum(onehot, axis=0, dtype=jnp.int32) - onehot
        counted = jnp.sum(before * onehot, axis=1, dtype=jnp.int32)
        slot_positions = jnp.where(counted < capacity, counted, -1).reshape(tok_rows, top_count)
        target = jnp.where(slot_positions >= 0, token_experts * capacity + slot_positions, -1)
        matched = target[None, :, :] == jnp.arange(slots_all, dtype=jnp.int32)[:, None, None]
        placing = jnp.any(matched, axis=2).astype(brain_float_half)
        slot_weight = jnp.sum(jnp.where(matched, combine_weight[None, :, :], 0.0), axis=(1, 2)).reshape(
            experts_all, capacity
        )
        whole_x, whole_dy = (
            lax.all_gather(activations, "tensor", axis=1, tiled=True),
            lax.all_gather(output_gradient, "tensor", axis=1, tiled=True),
        )
        d_whole = whole_x.shape[1]
        sent_x = (
            jnp.dot(placing, whole_x, preferred_element_type=single_float)
            .astype(brain_float_half)
            .reshape(experts_all, capacity, d_whole)
        )
        sent_dy = (
            jnp.dot(placing, whole_dy, preferred_element_type=single_float)
            .astype(brain_float_half)
            .reshape(experts_all, capacity, d_whole)
        )
        recv_x, recv_dy, recv_w = (
            lax.all_to_all(sent_x, "expert", split_axis=0, concat_axis=1, tiled=True),
            lax.all_to_all(sent_dy, "expert", split_axis=0, concat_axis=1, tiled=True),
            lax.all_to_all(
                slot_weight.astype(jnp.bfloat16), "expert", split_axis=0, concat_axis=1, tiled=True
            ).astype(slot_weight.dtype),
        )
    gradient_start = lax.axis_index("tensor") * gradient_slice
    gradient_listing = ([], [], [], [])
    input_rows = recv_x[0]
    dy_rows = recv_dy[0]
    gradient_rows = (recv_w[0][:, None] * dy_rows.astype(single_float)).astype(brain_float_half)
    scaled_gradient = (gradient_rows.astype(single_float) * down_channel_scale[0][None, :]).astype(
        brain_float_half
    )
    adapter_input_rows = jnp.dot(
        input_rows, adapter_input_first[0], preferred_element_type=single_float
    ).astype(brain_float_half)
    gate_values = (
        contract_product(input_rows, gate_up_weight[0, 0], 1, 1)
        * gate_up_channel_scale[0, 0][None, :]
    )
    gate_values = gate_values + ADAPTER_SCALE * jnp.dot(
        adapter_input_rows, adapter_input_second[0][:, 0, :], preferred_element_type=single_float
    )
    up_activation = (
        contract_product(input_rows, gate_up_weight[0, 1], 1, 1)
        * gate_up_channel_scale[0, 1][None, :]
    )
    up_activation = up_activation + ADAPTER_SCALE * jnp.dot(
        adapter_input_rows, adapter_input_second[0][:, 1, :], preferred_element_type=single_float
    )
    sig = jax.nn.sigmoid(ALPHA * gate_values)
    glu = gate_values * sig
    hidden_units = ((up_activation + 1.0) * glu).astype(brain_float_half)
    down_portion = jnp.dot(hidden_units, adapter_down_first[0], preferred_element_type=single_float)
    backward_adapter = contract_product(gradient_rows, adapter_down_second[0], 1, 1).astype(
        brain_float_half
    )
    hidden_gradient = contract_product(
        scaled_gradient, down_weight[0], 1, 1
    ) + ADAPTER_SCALE * contract_product(backward_adapter, adapter_down_first[0], 1, 1)
    d_up = hidden_gradient * glu
    d_gate = (
        hidden_gradient * (up_activation + 1.0) * sig * (1.0 + ALPHA * gate_values * (1.0 - sig))
    )
    d_both = jnp.stack([d_gate, d_up], axis=1)
    adapter_mid_gradient = d_both.astype(brain_float_half)
    dz_scaled = (d_both * gate_up_channel_scale[0][None, :, :]).astype(brain_float_half)
    input_portion = jnp.einsum(
        "ndy,tdy->nt",
        adapter_mid_gradient,
        adapter_input_second[0],
        preferred_element_type=single_float,
    )
    if dense:
        own_low = jnp.concatenate([down_portion.T, input_portion.T], axis=0).astype(jnp.bfloat16)
        pair_low = lax.ppermute(own_low, "tensor", [(0, 1), (1, 0)])
        low_sum = (own_low.astype(jnp.float32) + pair_low.astype(jnp.float32)).T
        down_sum, in_sum = jnp.split(low_sum, 2, axis=1)
    else:
        down_sum = lax.psum(down_portion.astype(jnp.bfloat16), "tensor").astype(jnp.float32)
        in_sum = lax.psum(input_portion.astype(jnp.bfloat16), "tensor").astype(jnp.float32)
    down_adapter = down_sum.astype(brain_float_half)
    input_adapter = in_sum.astype(brain_float_half)
    partial_value = jnp.einsum(
        "rjf,jfd->rd", dz_scaled, gate_up_weight[0], preferred_element_type=single_float
    )
    if dense:
        partial_rows = (
            partial_value
            + ADAPTER_SCALE
            * contract_product(input_portion.astype(brain_float_half), adapter_input_first[0], 1, 1)
        ).astype(brain_float_half)
    else:
        summed_values = lax.psum_scatter(
            partial_value.astype(jnp.bfloat16), "tensor", scatter_dimension=1, tiled=True
        ).astype(jnp.float32)
        input_first_rows = lax.dynamic_slice_in_dim(
            adapter_input_first[0], gradient_start, gradient_slice, 0
        )
        input_gradient_rows = (
            summed_values + ADAPTER_SCALE * contract_product(input_adapter, input_first_rows, 1, 1)
        ).astype(brain_float_half)
        dx_list = [input_gradient_rows]
    input_columns = lax.dynamic_slice_in_dim(input_rows, gradient_start, gradient_slice, 1)
    gradient_columns = lax.dynamic_slice_in_dim(gradient_rows, gradient_start, gradient_slice, 1)
    if dense:
        rank = input_adapter.shape[1]
        hidden_count = hidden_units.shape[1]
        wide = jnp.concatenate(
            [
                contract_product(input_adapter, input_columns, 0, 0),
                contract_product(down_adapter, gradient_columns, 0, 0),
            ],
            axis=0,
        )
        thin = jnp.concatenate(
            [
                contract_product(adapter_input_rows, adapter_mid_gradient[:, 0], 0, 0),
                contract_product(adapter_input_rows, adapter_mid_gradient[:, 1], 0, 0),
                contract_product(backward_adapter, hidden_units, 0, 0),
            ],
            axis=0,
        )
        input_grad, wide_sum, thin_sum = return_rows(
            partial_rows.T,
            (ADAPTER_SCALE * wide).astype(brain_float_half),
            (ADAPTER_SCALE * thin).astype(brain_float_half),
        )
        return (
            input_grad.T,
            wide_sum[:rank].T[None],
            jnp.stack([thin_sum[:rank], thin_sum[rank : 2 * rank]], axis=1)[None],
            thin_sum[2 * rank :].T[None],
            wide_sum[rank:][None],
        )
    gradient_listing[0].append(ADAPTER_SCALE * contract_product(input_columns, input_adapter, 0, 0))
    gradient_listing[1].append(
        ADAPTER_SCALE
        * jnp.einsum(
            "hp,hwl->pwl",
            adapter_input_rows,
            adapter_mid_gradient,
            preferred_element_type=single_float,
        )
    )
    gradient_listing[2].append(
        ADAPTER_SCALE * contract_product(hidden_units, backward_adapter, 0, 0)
    )
    gradient_listing[3].append(
        ADAPTER_SCALE * contract_product(down_adapter, gradient_columns, 0, 0)
    )
    stacked = tuple((jnp.stack(items, axis=0) for items in gradient_listing))
    input_first_gradient, input_second_gradient, down_first_gradient, down_second_gradient = (
        lax.psum(stacked[0].astype(jnp.bfloat16), "dp").astype(jnp.float32),
        lax.psum(stacked[1].astype(jnp.bfloat16), "dp").astype(jnp.float32),
        lax.psum(stacked[2].astype(jnp.bfloat16), "dp").astype(jnp.float32),
        lax.psum(stacked[3].astype(jnp.bfloat16), "dp").astype(jnp.float32),
    )
    returned = lax.all_to_all(
        jnp.stack(dx_list, axis=0), "expert", split_axis=1, concat_axis=0, tiled=True
    )
    flat_rows = returned.reshape(slots_all, gradient_slice)
    input_grad = contract_product(placing, flat_rows, 0, 0).astype(brain_float_half)
    return (
        input_grad,
        input_first_gradient,
        input_second_gradient,
        down_first_gradient,
        down_second_gradient,
    )


def solution(mesh):
    placed = (
        P(("dp", "expert"), "tensor"),
        P(("dp", "expert"), "tensor"),
        P(("dp", "expert"), None),
        P(("dp", "expert"), None),
        P("expert", None, "tensor", None),
        P("expert", None, "tensor"),
        P("expert", "tensor", None),
        P("expert", None),
        P("expert", None, None),
        P("expert", None, None, "tensor"),
        P("expert", "tensor", None),
        P("expert", None, None),
    )
    return jax.shard_map(
        shards,
        mesh=mesh,
        in_specs=placed,
        out_specs=(
            P(("dp", "expert"), "tensor"),
            P("expert", "tensor", None),
            P("expert", None, None, "tensor"),
            P("expert", "tensor", None),
            P("expert", None, "tensor"),
        ),
        check_vma=False,
    )
```
